128 devices in a mesh: ctx: 8 (over z_lo, y), grp: 16 (over z_hi, x, core).
Axes of the slice: x: 4, y: 4, z: 4 (z_hi: 2, z_lo: 2; z = z_hi * 2 + z_lo), core: 2. Of those that a mesh axis runs over, the one named last changes fastest.
Arguments:
- queries: bfloat16 [32, 6144], P('grp'), may hold values from -6 to 6
- key_cache: bfloat16 [32, 1024, 1024], P('grp', 'ctx'), may hold values from -6 to 6
- value_cache: bfloat16 [32, 1024, 1024], P('grp', 'ctx'), may hold values from -24 to 24
- new_key: bfloat16 [32, 1024], P('grp'), may hold values from -6 to 6
- new_value: bfloat16 [32, 1024], P('grp'), may hold values from -24 to 24
- lengths: int32 [32], P('grp'), may hold values from 2 to 1024, as said below
- moe_input: bfloat16 [512, 6144], P(('ctx', 'grp')), may hold values from -6 to 6
- routes: int32 [512, 4], P(('ctx', 'grp')), may hold values from 0 to 15, all different within a row; in each aligned block of 4 rows (0 to 3, 4 to 7, ...) at most 2 rows name the same one
- route_weights: float32 [512, 4], P(('ctx', 'grp')), may hold values from 0.05 to 1
- w_gate: bfloat16 [16, 6144, 5376], P('grp', None, 'ctx'), may hold values from -0.078125 to 0.078125
- w_up: bfloat16 [16, 6144, 5376], P('grp', None, 'ctx'), may hold values from -0.078125 to 0.078125
- w_down: bfloat16 [16, 5376, 6144], P('grp', 'ctx'), may hold values from -0.078125 to 0.078125
Outputs:
- head_outputs: bfloat16 [32, 6144], P('grp', 'ctx')
- expert_mix: bfloat16 [512, 6144], P(('ctx', 'grp'))
The draws below stay inside these ranges and needn't reach their ends.
Inputs may be any that keep to these rules, and one draw needn't show every extreme that they name: `routes`: each row names 4 different experts; among the 4 rows of one device no expert is named more than 2 times, and in every draw some expert is named exactly 2 times by the rows of one device. Row r attends to its cache positions below lengths[r] and to its new key; some row uses all 1024 positions.
All inputs are finite; a program needn't handle non-finite values.
Results may differ from the reference program's by a relative error of at most 0.02.
Values may be sent and summed in bfloat16 or wider, within the bound.
No kernel may reach another device: no remote copies, remote signals or barrier semaphores. Data moves between devices by JAX's collectives and lax.ppermute only.
A program may use at most 128 MiB of HBM per device.

```python
import math
import jax
import jax.numpy as jnp
import numpy as np
from jax import lax

D = 6144
QH = 48
KVH = 8
HD = 128
TOPK = 4
FF_WIN = 5376
RB_DEV = 4
E = 16
CAP = 2
FF_DEV = 672
CONTEXT = 1024
ROWS_A = 32
ROWS_B = 512
N_CTX = 8


def draw_queries(key, part):
    key = jax.random.fold_in(key, 1)
    drawn = 1.5 * jnp.clip(jax.random.normal(key, (ROWS_A, QH * HD), jnp.float32), -4.0, 4.0)
    return drawn.astype(jnp.bfloat16)


def draw_key_cache(key, part):
    key = jax.random.fold_in(key, 2)
    drawn = jnp.clip(jax.random.normal(key, (ROWS_A, CONTEXT, KVH * HD), jnp.float32), -6.0, 6.0)
    return drawn.astype(jnp.bfloat16)


def draw_lengths(key, part):
    key = jax.random.fold_in(key, 3)
    drawn = jax.random.randint(key, (ROWS_A,), 2, CONTEXT + 1)
    full_row = jax.random.randint(jax.random.fold_in(key, 1), (), 0, ROWS_A)
    short_row = (full_row + 1 + jax.random.randint(jax.random.fold_in(key, 2), (), 0, ROWS_A - 1)) % ROWS_A
    short_length = jax.random.randint(jax.random.fold_in(key, 4), (), 2, 6)
    drawn = drawn.at[short_row].set(short_length).at[full_row].set(CONTEXT)
    return drawn.astype(jnp.int32)


def shard_levels(own_key, shape, split, least, largest):
    def one(axis_at, shards_of):
        steps = jax.random.uniform(jax.random.fold_in(jax.random.fold_in(own_key, 6), axis_at), (shards_of,), jnp.float32, least / len(split), largest / len(split))
        return jnp.repeat(jnp.exp(steps), shape[axis_at] // shards_of).reshape((-1,) + (1,) * (len(shape) - axis_at - 1))

    gain = one(*split[0])
    for cut in split[1:]:
        gain = gain * one(*cut)
    return gain


def assign_block(stream_key, own, number, rows, number_of, top, limit, slope):
    sequence = jax.random.permutation(stream_key, number_of)
    packed, common = portions_of(number_of, rows * top, limit, slope, True), portions_of(number_of, rows * top, limit, slope, False)
    places = jnp.arange(number_of)

    def named(sizes, rotation):
        used = int((sizes > 0).sum())
        fixed = max(1, used // 4)
        shifted = fixed + (places - fixed + rotation * (used - fixed)) % max(1, number_of - fixed)
        return jnp.zeros((number_of,), jnp.int32).at[sequence[jnp.where(places < fixed, places, shifted)]].set(jnp.asarray(sizes, jnp.int32))

    sizes = jnp.where(number % 4 == 0, named(packed, number // 4), named(common, number - number // 4 - 1))
    mixed = jax.random.permutation(jax.random.fold_in(own, 3), number_of)
    donor, receiver = mixed[0:number_of // 2 * 2:2], mixed[1:number_of // 2 * 2:2]
    slack = jnp.minimum(sizes[donor] - 1, limit - sizes[receiver]) // 2
    slack = jnp.where((donor == sequence[0]) | (receiver == sequence[0]) | (sizes[receiver] == 0), 0, jnp.maximum(slack, 0))
    shifted = jax.random.randint(jax.random.fold_in(own, 4), (number_of // 2,), 0, 1 << 20) % (slack + 1)
    sizes = sizes.at[donor].add(-shifted).at[receiver].add(shifted)
    labels = jnp.searchsorted(jnp.cumsum(sizes), jnp.arange(rows * top), side="right").astype(jnp.int32)
    grid = labels.reshape(top, rows).T
    grid = grid[jax.random.permutation(jax.random.fold_in(own, 1), rows)]
    rotation = jax.random.randint(jax.random.fold_in(own, 2), (rows, 1), 0, top)
    return jnp.take_along_axis(grid, (jnp.arange(top)[None, :] + rotation) % top, axis=1)


def portions_of(amount, total, bound, lean, full):
    loads = [(1 << 20) // math.isqrt(rank ** lean) + 1 for rank in range(1, amount + 1)]
    largest = bound if full else min(bound, max(-(-total // amount), total * loads[0] // sum(loads)))
    least = 1 if total - largest >= amount - 1 else 0
    holding, spare = [largest] + [least] * (amount - 1), total - largest - least * (amount - 1)
    while spare > 0:
        candidates = [i for i in range(1, amount) if holding[i] < largest] or [i for i in range(1, amount) if holding[i] < bound]
        mass, remaining = sum([loads[i] for i in candidates]), spare
        for i in candidates:
            more = min(bound - holding[i], max(1, remaining * loads[i] // mass), spare)
            holding[i] = holding[i] + more
            spare = spare - more
    return np.array(holding)


def normal_values(rng, dims, scale, limit, cuts=(), held_as=jnp.bfloat16):
    values = scale * jax.random.normal(rng, dims, jnp.float32)
    if cuts:
        values = values * shard_levels(rng, dims, cuts, -0.22, 0.18)
    return jnp.clip(values, -limit, limit).astype(held_as)


def setup_inputs(seed: int = 0) -> dict:
    arg_keys = jax.random.split(jax.random.key(seed), 13)
    queries = draw_queries(jax.random.fold_in(arg_keys[12], 71), 0)
    key_cache = draw_key_cache(jax.random.fold_in(arg_keys[12], 71), 0)
    value_cache = normal_values(arg_keys[2], (ROWS_A, CONTEXT, KVH * HD), 4.0, 24.0, ((0, 16), (1, 8)))
    new_key = normal_values(arg_keys[3], (ROWS_A, KVH * HD), 1.0, 6.0, ((0, 16),))
    new_value = normal_values(arg_keys[4], (ROWS_A, KVH * HD), 4.0, 24.0, ((0, 16),))
    lengths = draw_lengths(jax.random.fold_in(arg_keys[12], 71), 0)
    moe_input = normal_values(arg_keys[6], (ROWS_B, D), 1.0, 6.0, ((0, 128),))
    routes_keys = jax.random.split(jax.random.fold_in(arg_keys[7], 1), ROWS_B // RB_DEV)
    routes_turns = jax.random.permutation(jax.random.fold_in(arg_keys[7], 3), ROWS_B // RB_DEV)
    routes = jax.vmap(lambda own, number: assign_block(jax.random.fold_in(arg_keys[7], 2), own, number, RB_DEV, E, TOPK, CAP, 2))(routes_keys, routes_turns).reshape((ROWS_B, TOPK))
    route_weights = jnp.clip(jnp.exp(math.log(1.0) - 2.9957323 * jax.random.uniform(arg_keys[8], (ROWS_B, TOPK), jnp.float32) ** shard_levels(arg_keys[8], (ROWS_B, TOPK), ((0, 128),), -0.2, 0.2)), 0.05, 1.0)
    w_gate = normal_values(arg_keys[9], (E, D, FF_WIN), D ** -0.5, 0.078125, ((0, 16), (2, 8)))
    w_up = normal_values(arg_keys[10], (E, D, FF_WIN), D ** -0.5, 0.078125, ((0, 16), (2, 8)))
    w_down = normal_values(arg_keys[11], (E, FF_WIN, D), FF_WIN ** -0.5, 0.078125, ((0, 16), (1, 8)))
    return dict(queries=queries, key_cache=key_cache, value_cache=value_cache, new_key=new_key, new_value=new_value, lengths=lengths, moe_input=moe_input, routes=routes, route_weights=route_weights, w_gate=w_gate, w_up=w_up, w_down=w_down)


def attend(queries, key_cache, value_cache, new_key, new_value, lengths):
    row_count = queries.shape[0]
    context = key_cache.shape[1]
    group = QH // KVH
    scale = HD ** -0.5
    high = lax.Precision.HIGHEST
    q_heads = queries.astype(jnp.float32).reshape(row_count, KVH, group, HD)
    keys_all = key_cache.astype(jnp.float32).reshape(row_count, context, KVH, HD)
    values_all = value_cache.astype(jnp.float32).reshape(row_count, context, KVH, HD)
    scores = jnp.einsum("rkgd,rckd->rkgc", q_heads, keys_all, precision=high) * scale
    own_keys = new_key.astype(jnp.float32).reshape(row_count, KVH, HD)
    own_score = jnp.einsum("rkgd,rkd->rkg", q_heads, own_keys, precision=high) * scale
    live = (jnp.arange(context, dtype=jnp.int32)[None, :] < lengths[:, None])[:, None, None, :]
    peak = jnp.maximum(jnp.max(jnp.where(live, scores, -jnp.inf), axis=-1), own_score)
    weights = jnp.where(live, jnp.exp(scores - peak[..., None]), 0.0)
    own_weight = jnp.exp(own_score - peak)
    total = jnp.sum(weights, axis=-1) + own_weight
    own_values = new_value.astype(jnp.float32).reshape(row_count, KVH, 1, HD)
    mixed = jnp.einsum("rkgc,rckd->rkgd", weights, values_all, precision=high) + own_weight[..., None] * own_values
    return (mixed / total[..., None]).reshape(row_count, QH * HD).astype(jnp.bfloat16)


def reference(queries, key_cache, value_cache, new_key, new_value, lengths, moe_input, routes, route_weights, w_gate, w_up, w_down):
    head_outputs = attend(queries, key_cache, value_cache, new_key, new_value, lengths)
    row_total = moe_input.shape[0]
    experts = w_gate.shape[0]
    blocks = row_total // RB_DEV
    flat = routes.reshape(blocks, RB_DEV * TOPK)
    onehot = (flat[..., None] == jnp.arange(experts, dtype=jnp.int32)[None, None, :]).astype(jnp.int32)
    earlier = jnp.cumsum(onehot, axis=1) - onehot
    slot_index = jnp.sum(earlier * onehot, axis=-1).astype(jnp.int32)
    place = flat * (blocks * CAP) + jnp.arange(blocks, dtype=jnp.int32)[:, None] * CAP + slot_index
    place = place.astype(jnp.int32)
    row_ids = jnp.repeat(jnp.arange(row_total, dtype=jnp.int32), TOPK).reshape(blocks, RB_DEV * TOPK)
    table = jnp.full((experts * blocks * CAP,), -1, jnp.int32).at[place.reshape(-1)].set(row_ids.reshape(-1))
    table = table.reshape(experts, blocks * CAP)

    def one_expert(items):
        ids, gate_w, up_w, down_w = items
        taken = ids >= 0
        picked_rows = jnp.where(taken[:, None], moe_input[jnp.maximum(ids, 0)], jnp.zeros((), jnp.bfloat16))
        gate = jnp.dot(picked_rows, gate_w, preferred_element_type=jnp.float32)
        upper = jnp.dot(picked_rows, up_w, preferred_element_type=jnp.float32)
        hidden = (jax.nn.silu(gate) * upper).astype(jnp.bfloat16)
        summed = jnp.zeros((ids.shape[0], D), jnp.float32)
        for block_id in range(N_CTX):
            lower = block_id * FF_DEV
            part = jnp.dot(hidden[:, lower:lower + FF_DEV], down_w[lower:lower + FF_DEV], preferred_element_type=jnp.float32)
            summed = summed + lax.optimization_barrier(part.astype(jnp.bfloat16)).astype(jnp.float32)
        return summed.astype(jnp.bfloat16)

    expert_rows = lax.map(one_expert, (table, w_gate, w_up, w_down))
    gathered = expert_rows.reshape(experts * blocks * CAP, D)[place.reshape(row_total, TOPK)].astype(jnp.float32)
    share = route_weights / jnp.sum(route_weights, axis=-1, keepdims=True)
    expert_mix = jnp.sum(share[..., None] * gathered, axis=1).astype(jnp.bfloat16)
    return head_outputs, expert_mix
```

```python
import functools

import jax
import jax.numpy as jnp
from jax import lax
from jax.experimental import pallas as pl
from jax.experimental.pallas import tpu as pltpu
from jax.sharding import PartitionSpec as P

QH = 48
KVH = 8
HD = 128
TOPK = 4
D = 6144
HALF = D // 2
FF = 672
META = 128
ALL = ("ctx", "grp")
BF = jnp.bfloat16
F32 = jnp.float32
KB = 512
STEPS = HALF // KB


def coords(i):
    c, g = divmod(i, 16)
    return {"x": (g >> 1) & 3, "y": c & 3, "z": ((g >> 3) << 1) | (c >> 2), "core": g & 1}


def index(x, y, z, core):
    return (((z & 1) << 2) | y) * 16 + (((z >> 1) << 3) | (x << 1) | core)


def shifted(axes, k):
    pairs = []
    for i in range(128):
        at = coords(i)
        axis = axes[at["core"]]
        at[axis] = (at[axis] + k) % (2 if axis == "core" else 4)
        pairs.append((i, index(**at)))
    return pairs


OUTER = ("x", "y")
INNER = ("y", "x")
CORE = ("core", "core")
COLUMNS = [
    [index(x, y, z, core) for z in range(4) for core in range(2)] for x in range(4) for y in range(4)
]


def move(a, axes, k):
    return lax.ppermute(a, ALL, shifted(axes, k % 4 if axes is not CORE else 1))


def turned(a):
    return a.reshape(4, 4, 16, a.shape[-1]).swapaxes(0, 1).reshape(a.shape)


def gate_up_kernel(core_ref, *refs):
    own, other = refs[0:4], refs[4:8]
    gate_w, up_w, out, gate, upper = refs[8:]
    step = pl.program_id(0)

    @pl.when(step == 0)
    def _():
        gate[...] = jnp.zeros_like(gate)
        upper[...] = jnp.zeros_like(upper)

    def add(rows):
        gate[...] += jnp.dot(rows, gate_w[...], preferred_element_type=F32)
        upper[...] += jnp.dot(rows, up_w[...], preferred_element_type=F32)

    @pl.when(step < STEPS)
    def _():
        add(jnp.concatenate([r[...] for r in own], axis=0))

    @pl.when(step >= STEPS)
    def _():
        add(turned(jnp.concatenate([r[...] for r in other], axis=0)))

    @pl.when(step == 2 * STEPS - 1)
    def _():
        v = gate[...]
        out[...] = (v / (1.0 + jnp.exp(-v)) * upper[...]).astype(BF)


def gate_up(core, own, other, gate_w, up_w):
    spec_own = pl.BlockSpec((64, KB), lambda i, c: (0, jnp.minimum(i, STEPS - 1)))
    spec_other = pl.BlockSpec((64, KB), lambda i, c: (0, jnp.maximum(i - STEPS, 0)))
    spec_w = pl.BlockSpec((KB, FF), lambda i, c: ((i + STEPS * c[0]) % (2 * STEPS), 0))
    return pl.pallas_call(
        gate_up_kernel,
        grid_spec=pltpu.PrefetchScalarGridSpec(
            num_scalar_prefetch=1,
            grid=(2 * STEPS,),
            in_specs=[spec_own] * 4 + [spec_other] * 4 + [spec_w] * 2,
            out_specs=pl.BlockSpec((256, FF), lambda i, c: (0, 0)),
            scratch_shapes=[pltpu.VMEM((256, FF), F32)] * 2,
        ),
        out_shape=jax.ShapeDtypeStruct((256, FF), BF),
        compiler_params=pltpu.CompilerParams(vmem_limit_bytes=40 << 20),
        cost_estimate=pl.CostEstimate(
            flops=4 * 256 * D * FF, bytes_accessed=4 * D * FF + 2 * 256 * D, transcendentals=256 * FF
        ),
        name="gate_up",
    )(core, *own, *other, gate_w, up_w)


def down_kernel(turn, half_ref, hidden, weights, share, out):
    rows = jnp.dot(hidden[...], weights[...], preferred_element_type=F32) * share[...]
    rows = rows.astype(BF)
    out[...] = turned(rows) if turn else rows


def down(half, hidden, weights, share, turn):
    return pl.pallas_call(
        functools.partial(down_kernel, turn),
        grid_spec=pltpu.PrefetchScalarGridSpec(
            num_scalar_prefetch=1,
            grid=(STEPS,),
            in_specs=[
                pl.BlockSpec((256, FF), lambda i, c: (0, 0)),
                pl.BlockSpec((FF, KB), lambda i, c: (0, i + STEPS * c[0])),
                pl.BlockSpec((256, 1), lambda i, c: (0, 0)),
            ],
            out_specs=pl.BlockSpec((256, KB), lambda i, c: (0, i)),
        ),
        out_shape=jax.ShapeDtypeStruct((256, HALF), BF),
        compiler_params=pltpu.CompilerParams(vmem_limit_bytes=40 << 20),
        cost_estimate=pl.CostEstimate(
            flops=2 * 256 * HALF * FF, bytes_accessed=2 * HALF * FF + 2 * 256 * HALF, transcendentals=0
        ),
        name="down",
    )(half, hidden, weights, share)


def attend_here(queries, key_cache, value_cache, new_key, new_value, lengths):
    rows, local = queries.shape[0], key_cache.shape[1]
    group = QH // KVH
    scale = HD ** (-0.5)
    q = queries.reshape(rows, KVH, group, HD)
    keys = key_cache.reshape(rows, local, KVH, HD)
    values = value_cache.reshape(rows, local, KVH, HD)
    scores = jnp.einsum("rkgd,rckd->rkgc", q, keys, preferred_element_type=F32) * scale
    own = (
        jnp.einsum("rkgd,rkd->rkg", q, new_key.reshape(rows, KVH, HD), preferred_element_type=F32)
        * scale
    )
    place = lax.axis_index("ctx")
    leader = place == 0
    position = place * local + jnp.arange(local, dtype=jnp.int32)
    live = (position[None, :] < lengths[:, None])[:, None, None, :]
    top = jnp.max(jnp.where(live, scores, -1e30), axis=-1)
    top = jnp.where(leader, jnp.maximum(top, own), top)
    top = lax.reduce_precision(top, 8, 7)
    weights = jnp.where(live, jnp.exp(scores - top[..., None]), 0.0)
    own_weight = jnp.where(leader, jnp.exp(own - top), 0.0)
    total = jnp.sum(weights, axis=-1) + own_weight
    high = lax.reduce_precision(weights, 8, 7)
    parts = jnp.concatenate([high.astype(BF), (weights - high).astype(BF)], axis=2)
    mixed = jnp.einsum("rkgc,rckd->rkgd", parts, values, preferred_element_type=F32)
    mixed = mixed[:, :, :group] + mixed[:, :, group:]
    mixed = mixed + own_weight[..., None] * new_value.reshape(rows, KVH, 1, HD).astype(F32)
    total_high = lax.reduce_precision(total, 8, 7)
    stats = jnp.stack([top, total_high, total - total_high], axis=-1).astype(BF)
    stats = jnp.pad(stats, ((0, 0), (0, 0), (0, 0), (0, HD - 3)))
    packed = jnp.concatenate([mixed.astype(BF), stats], axis=-1)
    return packed.transpose(1, 0, 2, 3).reshape(KVH, rows * group, 2 * HD)


def attend_join(parts):
    parts = parts.astype(F32)
    top = parts[:, :, HD]
    total = parts[:, :, HD + 1] + parts[:, :, HD + 2]
    scale = jnp.exp(top - jnp.max(top, axis=0, keepdims=True))
    joined = jnp.sum(parts[:, :, :HD] * scale[..., None], axis=0)
    joined = joined / jnp.sum(total * scale, axis=0)[:, None]
    group = QH // KVH
    return joined.reshape(-1, group * HD).astype(BF)


def describe(routes, route_weights):
    rows = routes.shape[0]
    same = routes[:, :, None, None] == routes[None, None, :, :]
    before = (jnp.arange(rows)[None, :] < jnp.arange(rows)[:, None])[:, None, :, None]
    slot = jnp.sum((same & before).astype(jnp.int32), axis=(2, 3))
    share = route_weights / jnp.sum(route_weights, axis=-1, keepdims=True)
    high = lax.reduce_precision(share, 8, 7)
    middle = lax.reduce_precision(share - high, 8, 7)
    low = share - high - middle
    columns = jnp.concatenate([routes.astype(F32), slot.astype(F32), high, middle, low], axis=1)
    return jnp.pad(columns, ((0, 0), (0, META - 5 * TOPK))).astype(BF)


def selection(meta, expert):
    meta = meta[:, : 5 * TOPK].astype(F32)
    hit = meta[:, :TOPK] == expert.astype(F32)
    slot = jnp.sum(jnp.where(hit, meta[:, TOPK : 2 * TOPK], 0.0), axis=1)
    share = meta[:, 2 * TOPK : 3 * TOPK] + meta[:, 3 * TOPK : 4 * TOPK] + meta[:, 4 * TOPK : 5 * TOPK]
    share = jnp.sum(jnp.where(hit, share, 0.0), axis=1)
    block = jnp.arange(128, dtype=jnp.int32) // 4
    target = jnp.where(jnp.any(hit, axis=1), block * 2 + slot.astype(jnp.int32), -1)
    chosen = target[None, :] == jnp.arange(64, dtype=jnp.int32)[:, None]
    return chosen.astype(BF), jnp.sum(jnp.where(chosen, share[None, :], 0.0), axis=1, keepdims=True)


def body(
    queries,
    key_cache,
    value_cache,
    new_key,
    new_value,
    lengths,
    moe_input,
    routes,
    route_weights,
    w_gate,
    w_up,
    w_down,
):
    expert = lax.axis_index("grp")
    core = expert % 2
    core_at = core.astype(jnp.int32).reshape(1)

    meta = describe(routes, route_weights)
    halves = moe_input.reshape(4, 2, HALF).swapaxes(0, 1)
    halves = jnp.concatenate([halves, jnp.broadcast_to(meta[None], (2, 4, META))], axis=2)
    sent = jnp.broadcast_to(halves[None], (4, 2, 4, HALF + META)).reshape(8, 4, HALF + META)
    column = lax.all_to_all(sent, ALL, 0, 0, axis_index_groups=COLUMNS, tiled=True)
    column = column.reshape(32, HALF + META)
    plane = jnp.concatenate([column] + [move(column, INNER, k) for k in (1, 2, 3)], axis=0)
    packed = attend_here(queries, key_cache, value_cache, new_key, new_value, lengths)
    plane, packed = lax.optimization_barrier((plane, packed))
    shards = [plane] + [move(plane, OUTER, k) for k in (1, 2, 3)]

    head_parts = lax.all_to_all(packed, "ctx", 0, 0, tiled=True)
    head_outputs = attend_join(head_parts)

    own, other, choose, shares = [], [], [], []
    for shard in shards:
        meta = shard[:, HALF:]
        mine, share = selection(meta, expert)
        theirs, _ = selection(meta, expert ^ 1)
        pick = jnp.concatenate([mine, theirs], axis=0)
        picked = jnp.dot(pick, shard[:, :HALF], preferred_element_type=F32).astype(BF)
        own.append(picked[:64])
        other.append(move(picked[64:], CORE, 1))
        choose.append(pick)
        shares.append(share)
    share = jnp.concatenate(shares, axis=0)

    hidden = gate_up(core_at, own, other, w_gate[0], w_up[0])
    theirs = down(1 - core_at, hidden, w_down[0], share, True)
    received = move(theirs, CORE, 1)
    mine = down(core_at, hidden, w_down[0], share, False)

    def back(k):
        rows = jnp.concatenate([mine[64 * k : 64 * k + 64], received[64 * k : 64 * k + 64]], axis=0)
        return lax.dot_general(
            choose[k], rows, (((0,), (0,)), ((), ())), preferred_element_type=F32
        ).astype(BF)

    def added(parts):
        return sum(p.astype(F32) for p in parts).astype(BF)

    plane = added([move(back(k), OUTER, -k) for k in (2, 1, 3)] + [back(0)])
    column = added(
        [move(plane[32 * k : 32 * k + 32], INNER, -k) for k in (2, 1, 3)] + [plane[:32]]
    )
    sums = lax.all_to_all(
        column.reshape(8, 4, HALF), ALL, 0, 0, axis_index_groups=COLUMNS, tiled=True
    )
    sums = jnp.sum(sums.reshape(4, 2, 4, HALF).astype(F32), axis=0).astype(BF)
    return head_outputs, sums.swapaxes(0, 1).reshape(4, D)


def solution(mesh):
    placed = (
        P("grp", None),
        P("grp", "ctx", None),
        P("grp", "ctx", None),
        P("grp", None),
        P("grp", None),
        P("grp"),
        P(ALL, None),
        P(ALL, None),
        P(ALL, None),
        P("grp", None, "ctx"),
        P("grp", None, "ctx"),
        P("grp", "ctx", None),
    )
    return jax.shard_map(
        body,
        mesh=mesh,
        in_specs=placed,
        out_specs=(P("grp", "ctx"), P(ALL, None)),
        check_vma=False,
    )
```

```python
import functools

import jax
import jax.numpy as jnp
from jax import lax
from jax.experimental import pallas as pl
from jax.experimental.pallas import tpu as pltpu
from jax.sharding import PartitionSpec as P

QH = 48
KVH = 8
HD = 128
TOPK = 4
D = 6144
HALF = D // 2
FF = 672
META = 128
OUT = 1
BACK = 2
OUT_WIDE = HALF // OUT
BACK_WIDE = HALF // BACK
KB = 512
OUT_STEPS = OUT_WIDE // KB
BACK_STEPS = BACK_WIDE // KB
ALL = ("ctx", "grp")
BF = jnp.bfloat16
F32 = jnp.float32


def coords(i):
    c, g = divmod(i, 16)
    return {"x": (g >> 1) & 3, "y": c & 3, "z": ((g >> 3) << 1) | (c >> 2), "core": g & 1}


def index(x, y, z, core):
    return (((z & 1) << 2) | y) * 16 + (((z >> 1) << 3) | (x << 1) | core)


def shifted(axes, k):
    pairs = []
    for i in range(128):
        at = coords(i)
        axis = axes[at["core"]]
        at[axis] = (at[axis] + k) % (2 if axis == "core" else 4)
        pairs.append((i, index(**at)))
    return pairs


OUTER = ("x", "y")
INNER = ("y", "x")
CORE = ("core", "core")
COLUMNS = [
    [index(x, y, z, core) for z in range(4) for core in range(2)] for x in range(4) for y in range(4)
]


def move(a, axes, k):
    return lax.ppermute(a, ALL, shifted(axes, k % 4 if axes is not CORE else 1))


def turned(a):
    return a.reshape(4, 4, 16, a.shape[-1]).swapaxes(0, 1).reshape(a.shape)


def call(kernel, outs, *args, name, limit=8, **kw):
    return pl.pallas_call(
        kernel,
        out_shape=outs,
        compiler_params=pltpu.CompilerParams(vmem_limit_bytes=limit << 20),
        cost_estimate=pl.CostEstimate(flops=0, bytes_accessed=0, transcendentals=0),
        name=name,
        **kw,
    )(*args)


VMEM = pl.BlockSpec(memory_space=pltpu.VMEM)
SMEM = pl.BlockSpec(memory_space=pltpu.SMEM)
HBM = pl.BlockSpec(memory_space=pltpu.HBM)


def in_hbm(*arrays):
    return [pltpu.with_memory_space_constraint(a, pltpu.HBM) for a in arrays]


def shape(*dims, dtype=BF):
    return jax.ShapeDtypeStruct(dims, dtype)


def pack_kernel(x_at, routes_at, weights_at, out, x, routes, weights, sems):
    copies = [
        pltpu.make_async_copy(a, b, sems.at[i])
        for i, (a, b) in enumerate(((x_at, x), (routes_at, routes), (weights_at, weights)))
    ]
    for copy in copies:
        copy.start()
    for copy in copies:
        copy.wait()
    row = lax.broadcasted_iota(jnp.int32, (4, TOPK), 0)
    place = lax.broadcasted_iota(jnp.int32, (4, TOPK), 1)
    named = jnp.zeros((4, TOPK), jnp.int32)
    for r in range(4):
        for k in range(TOPK):
            named = jnp.where((row == r) & (place == k), routes[r, k], named)
    code = 2 * named
    for r in range(3):
        for k in range(TOPK):
            code += jnp.where((named == routes[r, k]) & (row > r), 1, 0)
    share = weights[...] / jnp.sum(weights[...], axis=1, keepdims=True)
    high = share.astype(BF).astype(F32)
    middle = (share - high).astype(BF).astype(F32)
    lane = lax.broadcasted_iota(jnp.int32, (4, META), 1)
    meta = jnp.zeros((4, META), F32)
    for j, part in enumerate((code.astype(F32), high, middle, share - high - middle)):
        for k in range(TOPK):
            meta = jnp.where(lane == j * TOPK + k, part[:, k : k + 1], meta)
    meta = meta.astype(BF)
    for target in range(8):
        at = (target % 2) * HALF
        out[target, :, :OUT_WIDE] = x[:, at : at + OUT_WIDE]
        out[target, :, OUT_WIDE : OUT_WIDE + META] = meta
        if OUT > 1:
            out[target, :, OUT_WIDE + META :] = x[:, at + OUT_WIDE : at + HALF]


def pack(x, routes, weights):
    return call(
        pack_kernel,
        shape(8, 4, HALF + META),
        *in_hbm(x, routes, weights),
        name="pack",
        in_specs=[HBM] * 3,
        out_specs=VMEM,
        scratch_shapes=[
            pltpu.VMEM((4, D), BF),
            pltpu.SMEM((4, TOPK), jnp.int32),
            pltpu.VMEM((4, TOPK), F32),
            pltpu.SemaphoreType.DMA((3,)),
        ],
    )


def load_kernel(gate_at, up_at, down_at, gate, up, down, sems):
    parts = 3
    copies = []
    for i, (a, b) in enumerate(((gate_at, gate), (up_at, up), (down_at, down))):
        for p in range(parts):
            rows = pl.ds(p * (FF // parts), FF // parts)
            copies.append(pltpu.make_async_copy(a.at[rows], b.at[rows], sems.at[i, p]))
    for copy in copies:
        copy.start()
    for copy in copies:
        copy.wait()


def load(gate_w, up_w, down_w):
    return call(
        load_kernel,
        [pltpu.VMEM((FF, D), BF)] * 3,
        *in_hbm(gate_w, up_w, down_w),
        name="load",
        in_specs=[HBM] * 3,
        out_specs=[VMEM] * 3,
        scratch_shapes=[pltpu.SemaphoreType.DMA((3, 3))],
    )


def picked(chosen, rows, mine, theirs):
    for at in range(0, OUT_WIDE, KB):
        found = lax.dot_general(
            chosen, rows[:, at : at + KB], (((0,), (0,)), ((), ())), preferred_element_type=F32
        ).astype(BF)
        mine[:, at : at + KB] = found[:64]
        theirs[:, at : at + KB] = found[64:]


def choose_kernel(expert, rows, mine, theirs, chosen, shares):
    meta = rows[:, OUT_WIDE : OUT_WIDE + META].astype(F32)
    row = lax.broadcasted_iota(jnp.int32, (128, 128), 0)
    lane = lax.broadcasted_iota(jnp.int32, (128, 128), 1)
    wanted = 2 * jnp.where(lane < 64, expert[0], expert[0] ^ 1) + lane % 2
    wanted = jnp.where(row // 4 == (lane % 64) // 2, wanted, -1).astype(F32)
    ones = jnp.zeros((128, 128), F32)
    weighted = jnp.zeros((128, 128), F32)
    for k in range(TOPK):
        hit = meta[:, k : k + 1] == wanted
        share = sum(meta[:, j * TOPK + k : j * TOPK + k + 1] for j in (1, 2, 3))
        ones += jnp.where(hit, 1.0, 0.0)
        weighted += jnp.where(hit, share, 0.0)
    chosen[...] = ones.astype(BF)
    shares[...] = jnp.sum(weighted, axis=0, keepdims=True)
    picked(chosen[...], rows, mine, theirs)


def choose(expert, rows):
    return call(
        choose_kernel,
        [shape(64, OUT_WIDE), shape(64, OUT_WIDE), shape(128, 128), shape(1, 128, dtype=F32)],
        expert,
        rows,
        name="choose",
        in_specs=[SMEM, VMEM],
        out_specs=[VMEM] * 4,
    )


def pick_kernel(chosen, rows, mine, theirs):
    picked(chosen[...], rows, mine, theirs)


def pick(chosen, rows):
    return call(
        pick_kernel,
        [shape(64, OUT_WIDE), shape(64, OUT_WIDE)],
        chosen,
        rows,
        name="pick",
    )


def across(weights, rows):
    return lax.dot_general(weights, rows, (((1,), (1,)), ((), ())), preferred_element_type=F32)


def columns_of(half, chunk, wide):
    return pl.ds(pl.multiple_of(half * HALF + chunk * wide, wide), wide)


def own_kernel(chunk, core, *refs):
    own, gate_w, up_w, before, (gate, up) = refs[:4], refs[4], refs[5], refs[6:-2], refs[-2:]
    rows = jnp.concatenate([r[...] for r in own], axis=0)
    here = columns_of(core[0], chunk, OUT_WIDE)
    for out, weights, at in ((gate, gate_w, 0), (up, up_w, 1)):
        found = across(weights[:, here], rows)
        out[...] = found + before[at][...] if before else found


def other_kernel(chunk, peer, *refs):
    rows = turned(jnp.concatenate([r[...] for r in refs[:4]], axis=0))
    gate_w, up_w, gate_at, up_at, share, *outs = refs[4:]
    here = columns_of(peer[0], chunk, OUT_WIDE)
    gate = gate_at[...] + across(gate_w[:, here], rows)
    up = up_at[...] + across(up_w[:, here], rows)
    if chunk < OUT - 1:
        outs[0][...] = gate
        outs[1][...] = up
    else:
        hidden = gate / (1.0 + jnp.exp(-gate)) * up * share[...]
        outs[0][...] = hidden.T.astype(BF)


def gate_up(core, peer, chunk, own, other, gate_w, up_w, before, share):
    sums = [shape(FF, 256, dtype=F32)] * 2
    args = [core, *own, gate_w, up_w, *before]
    sums = call(
        functools.partial(own_kernel, chunk),
        sums,
        *args,
        name="gate_up_own",
        in_specs=[SMEM] + [VMEM] * (len(args) - 1),
        out_specs=[VMEM] * 2,
    )
    args = [peer, *other, gate_w, up_w, *sums, share]
    last = chunk == OUT - 1
    return call(
        functools.partial(other_kernel, chunk),
        shape(256, FF) if last else [shape(FF, 256, dtype=F32)] * 2,
        *args,
        name="gate_up_other",
        in_specs=[SMEM] + [VMEM] * (len(args) - 1),
        out_specs=VMEM if last else [VMEM] * 2,
    )


def down_kernel(chunk, turn, half, hidden, weights, out):
    here = columns_of(half[0], chunk, BACK_WIDE)
    rows = jnp.dot(hidden[...], weights[:, here], preferred_element_type=F32).astype(BF)
    out[...] = turned(rows) if turn else rows


def down(half, chunk, hidden, weights, turn):
    return call(
        functools.partial(down_kernel, chunk, turn),
        shape(256, BACK_WIDE),
        half,
        hidden,
        weights,
        name="down",
        in_specs=[SMEM, VMEM, VMEM],
        out_specs=VMEM,
    )


def give_kernel(chosen, mine, theirs, out):
    for at in range(0, BACK_WIDE, KB):
        rows = jnp.concatenate([mine[:, at : at + KB], theirs[:, at : at + KB]], axis=0)
        out[:, at : at + KB] = jnp.dot(chosen[...], rows, preferred_element_type=F32).astype(BF)


def give(chosen, mine, theirs, k):
    slots = pl.BlockSpec((64, BACK_WIDE), lambda i: (k, 0))
    return call(
        give_kernel,
        shape(128, BACK_WIDE),
        chosen,
        mine,
        theirs,
        name="give",
        grid=(1,),
        in_specs=[pl.BlockSpec((128, 128), lambda i: (0, 0)), slots, slots],
        out_specs=pl.BlockSpec((128, BACK_WIDE), lambda i: (0, 0)),
    )


def join_kernel(chosen, *refs):
    parts, outs = refs[:-4], refs[-4:]
    for c in range(BACK):
        mine, theirs, *arrived = parts[5 * c : 5 * c + 5]
        for at in range(0, BACK_WIDE, KB):
            here = slice(at, at + KB)
            rows = jnp.concatenate([mine[:, here], theirs[:, here]], axis=0)
            rows = jnp.dot(chosen[...], rows, preferred_element_type=F32)
            for part in arrived:
                rows += part[:, here].astype(F32)
            rows = rows.astype(BF)
            there = slice(c * BACK_WIDE + at, c * BACK_WIDE + at + KB)
            for k in range(4):
                outs[k][:, there] = rows[32 * k : 32 * k + 32]


def join(chosen, parts):
    slots = pl.BlockSpec((64, BACK_WIDE), lambda i: (0, 0))
    rows = pl.BlockSpec((128, BACK_WIDE), lambda i: (0, 0))
    return call(
        join_kernel,
        [shape(32, HALF)] * 4,
        chosen,
        *parts,
        name="join",
        grid=(1,),
        in_specs=[pl.BlockSpec((128, 128), lambda i: (0, 0))] + [slots, slots, rows, rows, rows] * BACK,
        out_specs=[pl.BlockSpec((32, HALF), lambda i: (0, 0))] * 4,
    )


def column_kernel(*refs):
    parts, out = refs[:-1], refs[-1]
    rows = sum(p[...].astype(F32) for p in parts).astype(BF)
    for target in range(8):
        out[target] = rows[4 * target : 4 * target + 4]


def last_kernel(parts, out):
    for core in range(2):
        rows = sum(parts[2 * z + core].astype(F32) for z in range(4))
        out[:, core * HALF : (core + 1) * HALF] = rows.astype(BF)


def attend_kernel(place, lengths_at, *refs):
    given, out, held, sems = refs[:5], refs[5], refs[6:12], refs[12]
    copies = [
        pltpu.make_async_copy(a, b, sems.at[i]) for i, (a, b) in enumerate(zip((lengths_at,) + given, held))
    ]
    for copy in copies:
        copy.start()
    for copy in copies:
        copy.wait()
    lengths, queries, keys, values, new_key, new_value = held
    group = QH // KVH
    local = keys.shape[1]
    leader = place[0] == 0
    position = place[0] * local + lax.broadcasted_iota(jnp.int32, (group, local), 1)
    lane = lax.broadcasted_iota(jnp.int32, (group, HD), 1)
    out[...] = jnp.zeros_like(out)
    for r in range(2):
        live = position < lengths[r]
        for j in range(KVH):
            head = slice(j * HD, (j + 1) * HD)
            q = queries[r, j]
            scores = across(q, keys[r, :, head]) * HD ** (-0.5)
            own = jnp.sum(
                q.astype(F32) * new_key[r : r + 1, head].astype(F32), axis=1, keepdims=True
            ) * HD ** (-0.5)
            top = jnp.max(jnp.where(live, scores, -1e30), axis=1, keepdims=True)
            top = jnp.where(leader, jnp.maximum(top, own), top)
            top = top.astype(BF).astype(F32)
            weights = jnp.where(live, jnp.exp(scores - top), 0.0)
            own = jnp.where(leader, jnp.exp(own - top), 0.0)
            total = jnp.sum(weights, axis=1, keepdims=True) + own
            high = weights.astype(BF)
            low = (weights - high.astype(F32)).astype(BF)
            value = values[r, :, head]
            mixed = jnp.dot(high, value, preferred_element_type=F32)
            mixed += jnp.dot(low, value, preferred_element_type=F32)
            mixed += own * new_value[r : r + 1, head].astype(F32)
            total_high = total.astype(BF).astype(F32)
            stats = jnp.where(lane == 0, top, jnp.where(lane == 1, total_high, total - total_high))
            out[j, 8 * r : 8 * r + group, :HD] = mixed.astype(BF)
            out[j, 8 * r : 8 * r + group, HD:] = stats.astype(BF)


def attend(queries, key_cache, value_cache, new_key, new_value, lengths):
    place = lax.axis_index("ctx").astype(jnp.int32).reshape(1)
    queries = queries.reshape(2, KVH, QH // KVH, HD)
    return call(
        attend_kernel,
        shape(KVH, 16, 2 * HD),
        place,
        *in_hbm(lengths, queries, key_cache, value_cache, new_key, new_value),
        name="attend",
        in_specs=[SMEM] + [HBM] * 6,
        out_specs=VMEM,
        scratch_shapes=[pltpu.SMEM((2,), jnp.int32)]
        + [pltpu.VMEM(a.shape, a.dtype) for a in (queries, key_cache, value_cache, new_key, new_value)]
        + [pltpu.SemaphoreType.DMA((6,))],
    )


def heads_kernel(parts, out):
    group = QH // KVH
    tops = [parts[s, :, HD : HD + 1].astype(F32) for s in range(KVH)]
    peak = functools.reduce(jnp.maximum, tops)
    mixed = jnp.zeros((16, HD), F32)
    total = jnp.zeros((16, 1), F32)
    for s in range(KVH):
        scale = jnp.exp(tops[s] - peak)
        mixed += scale * parts[s, :, :HD].astype(F32)
        total += scale * sum(parts[s, :, HD + i : HD + i + 1].astype(F32) for i in (1, 2))
    mixed = (mixed / total).astype(BF)
    for r in range(2):
        for g in range(group):
            out[r : r + 1, g * HD : (g + 1) * HD] = mixed[8 * r + g : 8 * r + g + 1]


def body(
    queries,
    key_cache,
    value_cache,
    new_key,
    new_value,
    lengths,
    moe_input,
    routes,
    route_weights,
    w_gate,
    w_up,
    w_down,
):
    expert = (lax.axis_index("grp") & 15).astype(jnp.int32)
    core = (expert & 1).reshape(1)
    expert = expert.reshape(1)

    packed = attend(queries, key_cache, value_cache, new_key, new_value, lengths)
    sent = pack(moe_input, routes, route_weights)
    column = lax.all_to_all(sent, ALL, 0, 0, axis_index_groups=COLUMNS, tiled=True)
    column, packed = lax.optimization_barrier((column, packed))
    column = column.reshape(32, HALF + META)
    head_parts = lax.all_to_all(packed, "ctx", 0, 0, tiled=True)
    plane = jnp.concatenate([column] + [move(column, INNER, k) for k in (1, 2, 3)], axis=0)
    cuts = [0] + [OUT_WIDE * (c + 1) + META for c in range(OUT)]
    planes = [plane[:, cuts[c] : cuts[c + 1]] for c in range(OUT)]

    weights = (w_gate[0].T, w_up[0].T, w_down[0])
    planes[0], head_parts, weights, expert, core, peer = lax.optimization_barrier(
        (planes[0], head_parts, weights, expert, core, 1 - core)
    )
    shards = [[p] + [move(p, OUTER, k) for k in (1, 2, 3)] for p in planes]
    gate_w, up_w, down_w = load(*weights)
    head_outputs = call(heads_kernel, shape(2, HD * QH // KVH), head_parts, name="heads")
    shards[-1][2], head_outputs, gate_w = lax.optimization_barrier(
        (shards[-1][2], head_outputs, gate_w)
    )

    chosen, shares, sums = [None] * 4, [None] * 4, ()
    for c in range(OUT):
        own, other = [None] * 4, [None] * 4
        for k in (0, 1, 3, 2):
            if c == 0:
                own[k], theirs, chosen[k], shares[k] = choose(expert, shards[c][k])
            else:
                own[k], theirs = pick(chosen[k], shards[c][k])
            other[k] = move(theirs, CORE, 1)
        share = jnp.concatenate([s[:, :64] for s in shares], axis=1)
        sums = gate_up(core, peer, c, own, other, gate_w, up_w, sums, share)
    hidden = sums

    parts = []
    for c in range(BACK):
        theirs = move(down(peer, c, hidden, down_w, True), CORE, 1)
        mine = down(core, c, hidden, down_w, False)
        parts += [mine, theirs]
        parts += [move(give(chosen[k], mine, theirs, k), OUTER, -k) for k in (2, 1, 3)]
    pieces = join(chosen[0], parts)
    pieces = [pieces[0]] + [move(pieces[k], INNER, -k) for k in (2, 1, 3)]
    column = call(column_kernel, shape(8, 4, HALF), *pieces, name="column")
    parts = lax.all_to_all(column, ALL, 0, 0, axis_index_groups=COLUMNS, tiled=True)
    return head_outputs, call(last_kernel, shape(4, D), parts, name="last")


def solution(mesh):
    placed = (
        P("grp", None),
        P("grp", "ctx", None),
        P("grp", "ctx", None),
        P("grp", None),
        P("grp", None),
        P("grp"),
        P(ALL, None),
        P(ALL, None),
        P(ALL, None),
        P("grp", None, "ctx"),
        P("grp", None, "ctx"),
        P("grp", "ctx", None),
    )
    return jax.shard_map(
        body,
        mesh=mesh,
        in_specs=placed,
        out_specs=(P("grp", "ctx"), P(ALL, None)),
        check_vma=False,
    )
```

```python
import functools

import jax
import jax.numpy as jnp
from jax import lax
from jax.experimental import pallas as pl
from jax.experimental.pallas import tpu as pltpu
from jax.sharding import PartitionSpec as P

QH = 48
KVH = 8
HD = 128
TOPK = 4
D = 6144
HALF = D // 2
FF = 672
META = 128
OUT = 1
BACK = 2
TIE = False
OUT_WIDE = HALF // OUT
BACK_WIDE = HALF // BACK
KB = 512
OUT_STEPS = OUT_WIDE // KB
BACK_STEPS = BACK_WIDE // KB
ALL = ("ctx", "grp")
BF = jnp.bfloat16
F32 = jnp.float32


def coords(i):
    c, g = divmod(i, 16)
    return {"x": (g >> 1) & 3, "y": c & 3, "z": ((g >> 3) << 1) | (c >> 2), "core": g & 1}


def index(x, y, z, core):
    return (((z & 1) << 2) | y) * 16 + (((z >> 1) << 3) | (x << 1) | core)


def shifted(axes, k):
    pairs = []
    for i in range(128):
        at = coords(i)
        axis = axes[at["core"]]
        at[axis] = (at[axis] + k) % (2 if axis == "core" else 4)
        pairs.append((i, index(**at)))
    return pairs


OUTER = ("x", "y")
INNER = ("y", "x")
CORE = ("core", "core")
PLANES = [
    [index(**{INNER[core]: i, OUTER[core]: o, "z": z, "core": core}) for i in range(4) for z in range(4)]
    for core in range(2)
    for o in range(4)
]


def move(a, axes, k):
    return lax.ppermute(a, ALL, shifted(axes, k % 4 if axes is not CORE else 1))


def turned(a):
    return a.reshape(4, 4, 16, a.shape[-1]).swapaxes(0, 1).reshape(a.shape)


def call(kernel, outs, *args, name, limit=8, **kw):
    return pl.pallas_call(
        kernel,
        out_shape=outs,
        compiler_params=pltpu.CompilerParams(vmem_limit_bytes=limit << 20),
        cost_estimate=pl.CostEstimate(flops=0, bytes_accessed=0, transcendentals=0),
        name=name,
        **kw,
    )(*args)


VMEM = pl.BlockSpec(memory_space=pltpu.VMEM)
SMEM = pl.BlockSpec(memory_space=pltpu.SMEM)
HBM = pl.BlockSpec(memory_space=pltpu.HBM)


def in_hbm(*arrays):
    return [pltpu.with_memory_space_constraint(a, pltpu.HBM) for a in arrays]


def shape(*dims, dtype=BF):
    return jax.ShapeDtypeStruct(dims, dtype)


def pack_kernel(core, x_at, routes_at, weights_at, keep, give, x, routes, weights, sems):
    copies = [
        pltpu.make_async_copy(a, b, sems.at[i])
        for i, (a, b) in enumerate(((x_at, x), (routes_at, routes), (weights_at, weights)))
    ]
    for copy in copies:
        copy.start()
    for copy in copies:
        copy.wait()
    row = lax.broadcasted_iota(jnp.int32, (4, TOPK), 0)
    place = lax.broadcasted_iota(jnp.int32, (4, TOPK), 1)
    named = jnp.zeros((4, TOPK), jnp.int32)
    for r in range(4):
        for k in range(TOPK):
            named = jnp.where((row == r) & (place == k), routes[r, k], named)
    code = 2 * named
    for r in range(3):
        for k in range(TOPK):
            code += jnp.where((named == routes[r, k]) & (row > r), 1, 0)
    share = weights[...] / jnp.sum(weights[...], axis=1, keepdims=True)
    high = share.astype(BF).astype(F32)
    middle = (share - high).astype(BF).astype(F32)
    lane = lax.broadcasted_iota(jnp.int32, (4, META), 1)
    meta = jnp.zeros((4, META), F32)
    for j, part in enumerate((code.astype(F32), high, middle, share - high - middle)):
        for k in range(TOPK):
            meta = jnp.where(lane == j * TOPK + k, part[:, k : k + 1], meta)
    meta = meta.astype(BF)
    own = jnp.where(core[0] == 0, x[:, :HALF], x[:, HALF:])
    other = jnp.where(core[0] == 0, x[:, HALF:], x[:, :HALF])
    for out, columns in ((keep, own), (give, other)):
        out[:, :OUT_WIDE] = columns[:, :OUT_WIDE]
        out[:, OUT_WIDE : OUT_WIDE + META] = meta
        if OUT > 1:
            out[:, OUT_WIDE + META :] = columns[:, OUT_WIDE:]


def pack(core, x, routes, weights):
    return call(
        pack_kernel,
        [shape(4, HALF + META)] * 2,
        core,
        *in_hbm(x, routes, weights),
        name="pack",
        in_specs=[SMEM] + [HBM] * 3,
        out_specs=[VMEM] * 2,
        scratch_shapes=[
            pltpu.VMEM((4, D), BF),
            pltpu.SMEM((4, TOPK), jnp.int32),
            pltpu.VMEM((4, TOPK), F32),
            pltpu.SemaphoreType.DMA((3,)),
        ],
    )


def spread_kernel(core, keep, got, out):
    first = jnp.where(core[0] == 0, keep[...], got[...])
    second = jnp.where(core[0] == 0, got[...], keep[...])
    rows = jnp.concatenate([first, second], axis=0)
    for target in range(16):
        out[target] = rows


def spread(core, keep, got):
    return call(
        spread_kernel,
        shape(16, 8, HALF + META),
        core,
        keep,
        got,
        name="spread",
        in_specs=[SMEM, VMEM, VMEM],
        out_specs=VMEM,
    )


def load_kernel(gate_at, up_at, down_at, gate, up, down, sems):
    parts = 3
    copies = []
    for i, (a, b) in enumerate(((gate_at, gate), (up_at, up), (down_at, down))):
        for p in range(parts):
            rows = pl.ds(p * (FF // parts), FF // parts)
            copies.append(pltpu.make_async_copy(a.at[rows], b.at[rows], sems.at[i, p]))
    for copy in copies:
        copy.start()
    for copy in copies:
        copy.wait()


def load(gate_w, up_w, down_w):
    return call(
        load_kernel,
        [pltpu.VMEM((FF, D), BF)] * 3,
        *in_hbm(gate_w, up_w, down_w),
        name="load",
        in_specs=[HBM] * 3,
        out_specs=[VMEM] * 3,
        scratch_shapes=[pltpu.SemaphoreType.DMA((3, 3))],
    )


def picked(chosen, rows, mine, theirs):
    for at in range(0, OUT_WIDE, KB):
        found = lax.dot_general(
            chosen, rows[:, at : at + KB], (((0,), (0,)), ((), ())), preferred_element_type=F32
        ).astype(BF)
        mine[:, at : at + KB] = found[:64]
        theirs[:, at : at + KB] = found[64:]


def choose_kernel(expert, place, rows, mine, theirs, chosen, shares):
    meta = rows[:, OUT_WIDE : OUT_WIDE + META].astype(F32)
    row = lax.broadcasted_iota(jnp.int32, (128, 128), 0)
    lane = lax.broadcasted_iota(jnp.int32, (128, 128), 1)
    wanted = 2 * jnp.where(lane < 64, expert[0], expert[0] ^ 1) + lane % 2
    block = ((place[0] - row // 32) & 3) * 8 + (row // 4) % 8
    wanted = jnp.where(block == (lane % 64) // 2, wanted, -1).astype(F32)
    ones = jnp.zeros((128, 128), F32)
    weighted = jnp.zeros((128, 128), F32)
    for k in range(TOPK):
        hit = meta[:, k : k + 1] == wanted
        share = sum(meta[:, j * TOPK + k : j * TOPK + k + 1] for j in (1, 2, 3))
        ones += jnp.where(hit, 1.0, 0.0)
        weighted += jnp.where(hit, share, 0.0)
    chosen[...] = ones.astype(BF)
    shares[...] = jnp.sum(weighted, axis=0, keepdims=True)
    picked(chosen[...], rows, mine, theirs)


def choose(expert, place, rows):
    return call(
        choose_kernel,
        [shape(64, OUT_WIDE), shape(64, OUT_WIDE), shape(128, 128), shape(1, 128, dtype=F32)],
        expert,
        place,
        rows,
        name="choose",
        in_specs=[SMEM, SMEM, VMEM],
        out_specs=[VMEM] * 4,
    )


def pick_kernel(chosen, rows, mine, theirs):
    picked(chosen[...], rows, mine, theirs)


def pick(chosen, rows):
    return call(
        pick_kernel,
        [shape(64, OUT_WIDE), shape(64, OUT_WIDE)],
        chosen,
        rows,
        name="pick",
    )


def across(weights, rows):
    return lax.dot_general(weights, rows, (((1,), (1,)), ((), ())), preferred_element_type=F32)


def columns_of(half, chunk, wide):
    return pl.ds(pl.multiple_of(half * HALF + chunk * wide, wide), wide)


def own_kernel(chunk, core, *refs):
    gate_w, up_w, gate, up = refs[4:]
    rows = jnp.concatenate([r[...] for r in refs[:4]], axis=0)
    here = columns_of(core[0], chunk, OUT_WIDE)
    gate[...] = across(gate_w[:, here], rows)
    up[...] = across(up_w[:, here], rows)


def gate_up_own(core, chunk, own, gate_w, up_w):
    return call(
        functools.partial(own_kernel, chunk),
        [shape(FF, 256, dtype=F32)] * 2,
        core,
        *own,
        gate_w,
        up_w,
        name="gate_up_own",
        in_specs=[SMEM] + [VMEM] * 6,
        out_specs=[VMEM] * 2,
    )


def hidden_kernel(peer, *refs):
    other, refs = refs[: 4 * OUT], refs[4 * OUT :]
    sums, refs = refs[: 2 * OUT], refs[2 * OUT :]
    gate_w, up_w, down_w, share, hidden, *theirs = refs
    gate = sum(r[...] for r in sums[0::2])
    up = sum(r[...] for r in sums[1::2])
    for c in range(OUT):
        rows = turned(jnp.concatenate([r[...] for r in other[4 * c : 4 * c + 4]], axis=0))
        here = columns_of(peer[0], c, OUT_WIDE)
        gate += across(gate_w[:, here], rows)
        up += across(up_w[:, here], rows)
    hidden[...] = (gate / (1.0 + jnp.exp(-gate)) * up * share[...]).T.astype(BF)
    for c in range(BACK):
        here = columns_of(peer[0], c, BACK_WIDE)
        rows = jnp.dot(hidden[...], down_w[:, here], preferred_element_type=F32)
        theirs[c][...] = turned(rows.astype(BF))


def hidden_rows(peer, other, sums, gate_w, up_w, down_w, share):
    args = [peer, *other, *sums, gate_w, up_w, down_w, share]
    return call(
        hidden_kernel,
        [shape(256, FF)] + [shape(256, BACK_WIDE)] * BACK,
        *args,
        name="hidden",
        in_specs=[SMEM] + [VMEM] * (len(args) - 1),
        out_specs=[VMEM] * (1 + BACK),
    )


def down_kernel(core, hidden, weights, *outs):
    for c in range(BACK):
        here = columns_of(core[0], c, BACK_WIDE)
        outs[c][...] = jnp.dot(hidden[...], weights[:, here], preferred_element_type=F32).astype(BF)


def down(core, hidden, weights):
    return call(
        down_kernel,
        [shape(256, BACK_WIDE)] * BACK,
        core,
        hidden,
        weights,
        name="down",
        in_specs=[SMEM, VMEM, VMEM],
        out_specs=[VMEM] * BACK,
    )


def give_kernel(chosen, mine, theirs, out):
    for at in range(0, BACK_WIDE, KB):
        rows = jnp.concatenate([mine[:, at : at + KB], theirs[:, at : at + KB]], axis=0)
        out[:, at : at + KB] = jnp.dot(chosen[...], rows, preferred_element_type=F32).astype(BF)


def give(chosen, mine, theirs, k):
    slots = pl.BlockSpec((64, BACK_WIDE), lambda i: (k, 0))
    return call(
        give_kernel,
        shape(128, BACK_WIDE),
        chosen,
        mine,
        theirs,
        name="give",
        grid=(1,),
        in_specs=[pl.BlockSpec((128, 128), lambda i: (0, 0)), slots, slots],
        out_specs=pl.BlockSpec((128, BACK_WIDE), lambda i: (0, 0)),
    )


def join_kernel(chosen, *refs):
    parts, out = refs[:-1], refs[-1]
    for c in range(BACK):
        mine, theirs, *arrived = parts[5 * c : 5 * c + 5]
        for at in range(0, BACK_WIDE, KB):
            here = slice(at, at + KB)
            rows = jnp.concatenate([mine[:, here], theirs[:, here]], axis=0)
            rows = jnp.dot(chosen[...], rows, preferred_element_type=F32)
            for part in arrived:
                rows += part[:, here].astype(F32)
            out[:, c * BACK_WIDE + at : c * BACK_WIDE + at + KB] = rows.astype(BF)


def join(chosen, parts):
    slots = pl.BlockSpec((64, BACK_WIDE), lambda i: (0, 0))
    rows = pl.BlockSpec((128, BACK_WIDE), lambda i: (0, 0))
    return call(
        join_kernel,
        shape(128, HALF),
        chosen,
        *parts,
        name="join",
        grid=(1,),
        in_specs=[pl.BlockSpec((128, 128), lambda i: (0, 0))] + [slots, slots, rows, rows, rows] * BACK,
        out_specs=pl.BlockSpec((128, HALF), lambda i: (0, 0)),
    )


def fold_kernel(core, parts, keep, give):
    rows = sum(parts[s].astype(F32) for s in range(16)).astype(BF)
    keep[...] = jnp.where(core[0] == 0, rows[:4], rows[4:])
    give[...] = jnp.where(core[0] == 0, rows[4:], rows[:4])


def fold(core, parts):
    return call(
        fold_kernel,
        [shape(4, HALF)] * 2,
        core,
        parts,
        name="fold",
        in_specs=[SMEM, VMEM],
        out_specs=[VMEM] * 2,
    )


def last_kernel(core, keep, got, out):
    out[:, :HALF] = jnp.where(core[0] == 0, keep[...], got[...])
    out[:, HALF:] = jnp.where(core[0] == 0, got[...], keep[...])


def attend_kernel(place, lengths_at, *refs):
    given, out, held, sems = refs[:5], refs[5], refs[6:12], refs[12]
    copies = [
        pltpu.make_async_copy(a, b, sems.at[i]) for i, (a, b) in enumerate(zip((lengths_at,) + given, held))
    ]
    for copy in copies:
        copy.start()
    for copy in copies:
        copy.wait()
    lengths, queries, keys, values, new_key, new_value = held
    group = QH // KVH
    local = keys.shape[1]
    leader = place[0] == 0
    position = place[0] * local + lax.broadcasted_iota(jnp.int32, (group, local), 1)
    lane = lax.broadcasted_iota(jnp.int32, (group, HD), 1)
    out[...] = jnp.zeros_like(out)
    for r in range(2):
        live = position < lengths[r]
        for j in range(KVH):
            head = slice(j * HD, (j + 1) * HD)
            q = queries[r, j]
            scores = across(q, keys[r, :, head]) * HD ** (-0.5)
            own = jnp.sum(
                q.astype(F32) * new_key[r : r + 1, head].astype(F32), axis=1, keepdims=True
            ) * HD ** (-0.5)
            top = jnp.max(jnp.where(live, scores, -1e30), axis=1, keepdims=True)
            top = jnp.where(leader, jnp.maximum(top, own), top)
            top = top.astype(BF).astype(F32)
            weights = jnp.where(live, jnp.exp(scores - top), 0.0)
            own = jnp.where(leader, jnp.exp(own - top), 0.0)
            total = jnp.sum(weights, axis=1, keepdims=True) + own
            high = weights.astype(BF)
            low = (weights - high.astype(F32)).astype(BF)
            value = values[r, :, head]
            mixed = jnp.dot(high, value, preferred_element_type=F32)
            mixed += jnp.dot(low, value, preferred_element_type=F32)
            mixed += own * new_value[r : r + 1, head].astype(F32)
            total_high = total.astype(BF).astype(F32)
            stats = jnp.where(lane == 0, top, jnp.where(lane == 1, total_high, total - total_high))
            out[j, 8 * r : 8 * r + group, :HD] = mixed.astype(BF)
            out[j, 8 * r : 8 * r + group, HD:] = stats.astype(BF)


def attend(queries, key_cache, value_cache, new_key, new_value, lengths):
    place = lax.axis_index("ctx").astype(jnp.int32).reshape(1)
    queries = queries.reshape(2, KVH, QH // KVH, HD)
    return call(
        attend_kernel,
        shape(KVH, 16, 2 * HD),
        place,
        *in_hbm(lengths, queries, key_cache, value_cache, new_key, new_value),
        name="attend",
        in_specs=[SMEM] + [HBM] * 6,
        out_specs=VMEM,
        scratch_shapes=[pltpu.SMEM((2,), jnp.int32)]
        + [pltpu.VMEM(a.shape, a.dtype) for a in (queries, key_cache, value_cache, new_key, new_value)]
        + [pltpu.SemaphoreType.DMA((6,))],
    )


def heads_kernel(parts, out):
    group = QH // KVH
    tops = [parts[s, :, HD : HD + 1].astype(F32) for s in range(KVH)]
    peak = functools.reduce(jnp.maximum, tops)
    mixed = jnp.zeros((16, HD), F32)
    total = jnp.zeros((16, 1), F32)
    for s in range(KVH):
        scale = jnp.exp(tops[s] - peak)
        mixed += scale * parts[s, :, :HD].astype(F32)
        total += scale * sum(parts[s, :, HD + i : HD + i + 1].astype(F32) for i in (1, 2))
    mixed = (mixed / total).astype(BF)
    for r in range(2):
        for g in range(group):
            out[r : r + 1, g * HD : (g + 1) * HD] = mixed[8 * r + g : 8 * r + g + 1]


def body(
    queries,
    key_cache,
    value_cache,
    new_key,
    new_value,
    lengths,
    moe_input,
    routes,
    route_weights,
    w_gate,
    w_up,
    w_down,
):
    expert = (lax.axis_index("grp") & 15).astype(jnp.int32)
    core, peer = expert & 1, 1 - (expert & 1)
    place = jnp.where(core == 0, lax.axis_index("ctx") & 3, (expert >> 1) & 3).astype(jnp.int32)
    expert, core, peer, place = (a.reshape(1) for a in (expert, core, peer, place))

    keep, sent = pack(core, moe_input, routes, route_weights)
    column = spread(core, keep, move(sent, CORE, 1))
    plane = lax.all_to_all(column, ALL, 0, 0, axis_index_groups=PLANES, tiled=True)
    packed = attend(queries, key_cache, value_cache, new_key, new_value, lengths)
    weights = (w_gate[0].T, w_up[0].T, w_down[0])
    plane, packed, weights, expert, core, peer, place = lax.optimization_barrier(
        (plane, packed, weights, expert, core, peer, place)
    )
    plane = plane.reshape(128, HALF + META)
    cuts = [0] + [OUT_WIDE * (c + 1) + META for c in range(OUT)]
    planes = [plane[:, cuts[c] : cuts[c + 1]] for c in range(OUT)]
    shards = [[p] + [move(p, OUTER, k) for k in (1, 2, 3)] for p in planes]

    gate_w, up_w, down_w = load(*weights)
    shards[0][1], gate_w = lax.optimization_barrier((shards[0][1], gate_w))

    chosen, shares, others, sums = [None] * 4, [None] * 4, [], []
    for c in range(OUT):
        own, other = [None] * 4, [None] * 4
        for k in (0, 1, 3, 2):
            if c == 0:
                own[k], theirs, chosen[k], shares[k] = choose(expert, place, shards[c][k])
            else:
                own[k], theirs = pick(chosen[k], shards[c][k])
            other[k] = move(theirs, CORE, 1)
        others += other
        sums += gate_up_own(core, c, own, gate_w, up_w)
        if TIE and c < OUT - 1:
            sums, chosen = lax.optimization_barrier((sums, chosen))
    share = jnp.concatenate([s[:, :64] for s in shares], axis=1)
    hidden, *theirs = hidden_rows(peer, others, sums, gate_w, up_w, down_w, share)

    theirs = [move(t, CORE, 1) for t in theirs]
    mine = down(core, hidden, down_w)
    parts = []
    for c in range(BACK):
        given = [give(chosen[k], mine[c], theirs[c], k) for k in (1, 3, 2)]
        if c == BACK - 1:
            given[-1], packed = lax.optimization_barrier((given[-1], packed))
        parts += [mine[c], theirs[c]] + [move(g, OUTER, -k) for g, k in zip(given, (1, 3, 2))]

    head_parts = lax.all_to_all(packed, "ctx", 0, 0, tiled=True)
    parts[-1], head_parts = lax.optimization_barrier((parts[-1], head_parts))
    head_outputs = call(heads_kernel, shape(2, HD * QH // KVH), head_parts, name="heads")
    rows = join(chosen[0], parts).reshape(16, 8, HALF)
    keep, sent = fold(core, lax.all_to_all(rows, ALL, 0, 0, axis_index_groups=PLANES, tiled=True))
    mixed = call(
        last_kernel,
        shape(4, D),
        core,
        keep,
        move(sent, CORE, 1),
        name="last",
        in_specs=[SMEM, VMEM, VMEM],
        out_specs=VMEM,
    )
    return head_outputs, mixed


def solution(mesh):
    placed = (
        P("grp", None),
        P("grp", "ctx", None),
        P("grp", "ctx", None),
        P("grp", None),
        P("grp", None),
        P("grp"),
        P(ALL, None),
        P(ALL, None),
        P(ALL, None),
        P("grp", None, "ctx"),
        P("grp", None, "ctx"),
        P("grp", "ctx", None),
    )
    return jax.shard_map(
        body,
        mesh=mesh,
        in_specs=placed,
        out_specs=(P("grp", "ctx"), P(ALL, None)),
        check_vma=False,
    )
```

```python
import functools

import jax
import jax.numpy as jnp
from jax import lax
from jax.experimental import pallas as pl
from jax.experimental.pallas import tpu as pltpu
from jax.sharding import PartitionSpec as P

QH = 48
KVH = 8
HD = 128
TOPK = 4
D = 6144
HALF = D // 2
FF = 672
META = 128
KB = 512
ALL = ("ctx", "grp")
BF = jnp.bfloat16
F32 = jnp.float32


def coords(i):
    c, g = divmod(i, 16)
    return {"x": (g >> 1) & 3, "y": c & 3, "z": ((g >> 3) << 1) | (c >> 2), "core": g & 1}


def index(x, y, z, core):
    return (((z & 1) << 2) | y) * 16 + (((z >> 1) << 3) | (x << 1) | core)


def shifted(axes, k):
    pairs = []
    for i in range(128):
        at = coords(i)
        axis = axes[at["core"]]
        at[axis] = (at[axis] + k) % (2 if axis == "core" else 4)
        pairs.append((i, index(**at)))
    return pairs


OUTER = ("x", "y")
INNER = ("y", "x")
CORE = ("core", "core")
PLANES = [
    [index(**{INNER[core]: i, OUTER[core]: o, "z": z, "core": core}) for i in range(4) for z in range(4)]
    for core in range(2)
    for o in range(4)
]


def move(a, axes, k):
    return lax.ppermute(a, ALL, shifted(axes, k % 4 if axes is not CORE else 1))


def call(kernel, outs, *args, name, limit=8, **kw):
    return pl.pallas_call(
        kernel,
        out_shape=outs,
        compiler_params=pltpu.CompilerParams(vmem_limit_bytes=limit << 20),
        cost_estimate=pl.CostEstimate(flops=0, bytes_accessed=0, transcendentals=0),
        name=name,
        **kw,
    )(*args)


VMEM = pl.BlockSpec(memory_space=pltpu.VMEM)
SMEM = pl.BlockSpec(memory_space=pltpu.SMEM)
HBM = pl.BlockSpec(memory_space=pltpu.HBM)


def in_hbm(*arrays):
    return [pltpu.with_memory_space_constraint(a, pltpu.HBM) for a in arrays]


def shape(*dims, dtype=BF):
    return jax.ShapeDtypeStruct(dims, dtype)


def pack_kernel(x_at, routes_at, weights_at, out, x, routes, weights, sems):
    copies = [
        pltpu.make_async_copy(a, b, sems.at[i])
        for i, (a, b) in enumerate(((x_at, x), (routes_at, routes), (weights_at, weights)))
    ]
    for copy in copies:
        copy.start()
    for copy in copies:
        copy.wait()
    row = lax.broadcasted_iota(jnp.int32, (4, TOPK), 0)
    place = lax.broadcasted_iota(jnp.int32, (4, TOPK), 1)
    named = jnp.zeros((4, TOPK), jnp.int32)
    for r in range(4):
        for k in range(TOPK):
            named = jnp.where((row == r) & (place == k), routes[r, k], named)
    code = 2 * named
    for r in range(3):
        for k in range(TOPK):
            code += jnp.where((named == routes[r, k]) & (row > r), 1, 0)
    share = weights[...] / jnp.sum(weights[...], axis=1, keepdims=True)
    high = share.astype(BF).astype(F32)
    middle = (share - high).astype(BF).astype(F32)
    lane = lax.broadcasted_iota(jnp.int32, (4, META), 1)
    meta = jnp.zeros((4, META), F32)
    for j, part in enumerate((code.astype(F32), high, middle, share - high - middle)):
        for k in range(TOPK):
            meta = jnp.where(lane == j * TOPK + k, part[:, k : k + 1], meta)
    meta = meta.astype(BF)
    for target in range(16):
        out[target, :, :D] = x[...]
        out[target, :, D:] = meta


def pack(x, routes, weights):
    return call(
        pack_kernel,
        shape(16, 4, D + META),
        *in_hbm(x, routes, weights),
        name="pack",
        in_specs=[HBM] * 3,
        out_specs=VMEM,
        scratch_shapes=[
            pltpu.VMEM((4, D), BF),
            pltpu.SMEM((4, TOPK), jnp.int32),
            pltpu.VMEM((4, TOPK), F32),
            pltpu.SemaphoreType.DMA((3,)),
        ],
    )


def load_kernel(gate_at, up_at, down_at, gate, up, down, sems):
    parts = 3
    copies = []
    for i, (a, b) in enumerate(((gate_at, gate), (up_at, up), (down_at, down))):
        for p in range(parts):
            rows = pl.ds(p * (FF // parts), FF // parts)
            copies.append(pltpu.make_async_copy(a.at[rows], b.at[rows], sems.at[i, p]))
    for copy in copies:
        copy.start()
    for copy in copies:
        copy.wait()


def load(gate_w, up_w, down_w):
    return call(
        load_kernel,
        [pltpu.VMEM((FF, D), BF)] * 3,
        *in_hbm(gate_w, up_w, down_w),
        name="load",
        in_specs=[HBM] * 3,
        out_specs=[VMEM] * 3,
        scratch_shapes=[pltpu.SemaphoreType.DMA((3, 3))],
    )


def choose_kernel(expert, rows, mine, theirs, chosen):
    meta = rows[:, D:].astype(F32)
    row = lax.broadcasted_iota(jnp.int32, (64, 64), 0)
    lane = lax.broadcasted_iota(jnp.int32, (64, 64), 1)
    wanted = 2 * jnp.where(lane < 32, expert[0], expert[0] ^ 1) + lane % 2
    wanted = jnp.where(row // 4 == (lane % 32) // 2, wanted, -1).astype(F32)
    ones = jnp.zeros((64, 64), F32)
    for k in range(TOPK):
        ones += jnp.where(meta[:, k : k + 1] == wanted, 1.0, 0.0)
    chosen[...] = ones.astype(BF)
    for at in range(0, D + META, KB):
        here = slice(at, min(at + KB, D + META))
        found = lax.dot_general(
            chosen[...], rows[:, here], (((0,), (0,)), ((), ())), preferred_element_type=F32
        ).astype(BF)
        mine[:, here] = found[:32]
        theirs[:, here] = found[32:]


def choose(expert, rows):
    return call(
        choose_kernel,
        [shape(32, D + META), shape(32, D + META), shape(64, 64)],
        expert,
        rows,
        name="choose",
        in_specs=[SMEM, VMEM],
        out_specs=[VMEM] * 3,
    )


def across(weights, rows):
    return lax.dot_general(weights, rows, (((1,), (1,)), ((), ())), preferred_element_type=F32)


def expert_kernel(expert, *refs):
    picked, (gate_w, up_w, down_w, *outs) = refs[:8], refs[8:]
    rows = jnp.concatenate([r[:, :D] for r in picked], axis=0)
    meta = jnp.concatenate([r[:, D:] for r in picked], axis=0).astype(F32)
    share = jnp.zeros((256, 1), F32)
    for k in range(TOPK):
        of_row = sum(meta[:, j * TOPK + k : j * TOPK + k + 1] for j in (1, 2, 3))
        slot = meta[:, k : k + 1] - (2 * expert[0]).astype(F32)
        share += jnp.where((slot == 0.0) | (slot == 1.0), of_row, 0.0)
    gate, up = across(gate_w[...], rows), across(up_w[...], rows)
    hidden = ((gate / (1.0 + jnp.exp(-gate)) * up).T * share).astype(BF)
    for c in range(2):
        here = slice(c * HALF, (c + 1) * HALF)
        rows = jnp.dot(hidden, down_w[:, here], preferred_element_type=F32).astype(BF)
        outs[2 * c][...] = rows[:128]
        outs[2 * c + 1][...] = rows[128:]


def expert_rows(expert, own, other, gate_w, up_w, down_w):
    return call(
        expert_kernel,
        [shape(128, HALF)] * 4,
        expert,
        *own,
        *other,
        gate_w,
        up_w,
        down_w,
        name="expert",
        limit=16,
        in_specs=[SMEM] + [VMEM] * 11,
        out_specs=[VMEM] * 4,
    )


def given(chosen, mine, theirs, at):
    here = slice(at, at + KB)
    rows = jnp.concatenate([mine[:, here], theirs[:, here]], axis=0)
    return jnp.dot(chosen[...], rows, preferred_element_type=F32)


def give_kernel(chosen, mine, theirs, out):
    for at in range(0, HALF, KB):
        out[:, at : at + KB] = given(chosen, mine, theirs, at).astype(BF)


def give(chosen, mine, theirs, k):
    slots = pl.BlockSpec((32, HALF), lambda i: (k, 0))
    return call(
        give_kernel,
        shape(64, HALF),
        chosen,
        mine,
        theirs,
        name="give",
        grid=(1,),
        in_specs=[pl.BlockSpec((64, 64), lambda i: (0, 0)), slots, slots],
        out_specs=pl.BlockSpec((64, HALF), lambda i: (0, 0)),
    )


def join_kernel(chosen, *refs):
    parts, out = refs[:-1], refs[-1]
    for c in range(2):
        mine, theirs, *arrived = parts[5 * c : 5 * c + 5]
        for at in range(0, HALF, KB):
            rows = given(chosen, mine, theirs, at)
            for part in arrived:
                rows += part[:, at : at + KB].astype(F32)
            rows = rows.astype(BF)
            for block in range(16):
                out[block, :, c * HALF + at : c * HALF + at + KB] = rows[4 * block : 4 * block + 4]


def join(chosen, parts):
    slots = pl.BlockSpec((32, HALF), lambda i: (0, 0))
    rows = pl.BlockSpec((64, HALF), lambda i: (0, 0))
    return call(
        join_kernel,
        shape(16, 4, D),
        chosen,
        *parts,
        name="join",
        grid=(1,),
        in_specs=[pl.BlockSpec((64, 64), lambda i: (0, 0))] + [slots, slots, rows, rows, rows] * 2,
        out_specs=pl.BlockSpec((16, 4, D), lambda i: (0, 0, 0)),
    )


def fold_kernel(parts, out):
    out[...] = sum(parts[s].astype(F32) for s in range(16)).astype(BF)


def attend_kernel(place, lengths_at, *refs):
    given, out, held, sems = refs[:5], refs[5], refs[6:12], refs[12]
    copies = [
        pltpu.make_async_copy(a, b, sems.at[i]) for i, (a, b) in enumerate(zip((lengths_at,) + given, held))
    ]
    for copy in copies:
        copy.start()
    for copy in copies:
        copy.wait()
    lengths, queries, keys, values, new_key, new_value = held
    group = QH // KVH
    local = keys.shape[1]
    leader = place[0] == 0
    position = place[0] * local + lax.broadcasted_iota(jnp.int32, (group, local), 1)
    lane = lax.broadcasted_iota(jnp.int32, (group, HD), 1)
    out[...] = jnp.zeros_like(out)
    for r in range(2):
        live = position < lengths[r]
        for j in range(KVH):
            head = slice(j * HD, (j + 1) * HD)
            q = queries[r, j]
            scores = across(q, keys[r, :, head]) * HD ** (-0.5)
            own = jnp.sum(
                q.astype(F32) * new_key[r : r + 1, head].astype(F32), axis=1, keepdims=True
            ) * HD ** (-0.5)
            top = jnp.max(jnp.where(live, scores, -1e30), axis=1, keepdims=True)
            top = jnp.where(leader, jnp.maximum(top, own), top)
            top = top.astype(BF).astype(F32)
            weights = jnp.where(live, jnp.exp(scores - top), 0.0)
            own = jnp.where(leader, jnp.exp(own - top), 0.0)
            total = jnp.sum(weights, axis=1, keepdims=True) + own
            high = weights.astype(BF)
            low = (weights - high.astype(F32)).astype(BF)
            value = values[r, :, head]
            mixed = jnp.dot(high, value, preferred_element_type=F32)
            mixed += jnp.dot(low, value, preferred_element_type=F32)
            mixed += own * new_value[r : r + 1, head].astype(F32)
            total_high = total.astype(BF).astype(F32)
            stats = jnp.where(lane == 0, top, jnp.where(lane == 1, total_high, total - total_high))
            out[j, 8 * r : 8 * r + group, :HD] = mixed.astype(BF)
            out[j, 8 * r : 8 * r + group, HD:] = stats.astype(BF)


def attend(queries, key_cache, value_cache, new_key, new_value, lengths):
    place = lax.axis_index("ctx").astype(jnp.int32).reshape(1)
    queries = queries.reshape(2, KVH, QH // KVH, HD)
    return call(
        attend_kernel,
        shape(KVH, 16, 2 * HD),
        place,
        *in_hbm(lengths, queries, key_cache, value_cache, new_key, new_value),
        name="attend",
        in_specs=[SMEM] + [HBM] * 6,
        out_specs=VMEM,
        scratch_shapes=[pltpu.SMEM((2,), jnp.int32)]
        + [pltpu.VMEM(a.shape, a.dtype) for a in (queries, key_cache, value_cache, new_key, new_value)]
        + [pltpu.SemaphoreType.DMA((6,))],
    )


def heads_kernel(parts, out):
    group = QH // KVH
    tops = [parts[s, :, HD : HD + 1].astype(F32) for s in range(KVH)]
    peak = functools.reduce(jnp.maximum, tops)
    mixed = jnp.zeros((16, HD), F32)
    total = jnp.zeros((16, 1), F32)
    for s in range(KVH):
        scale = jnp.exp(tops[s] - peak)
        mixed += scale * parts[s, :, :HD].astype(F32)
        total += scale * sum(parts[s, :, HD + i : HD + i + 1].astype(F32) for i in (1, 2))
    mixed = (mixed / total).astype(BF)
    for r in range(2):
        for g in range(group):
            out[r : r + 1, g * HD : (g + 1) * HD] = mixed[8 * r + g : 8 * r + g + 1]


def body(
    queries,
    key_cache,
    value_cache,
    new_key,
    new_value,
    lengths,
    moe_input,
    routes,
    route_weights,
    w_gate,
    w_up,
    w_down,
):
    expert = lax.axis_index("grp").astype(jnp.int32).reshape(1)

    sent = pack(moe_input, routes, route_weights)
    plane = lax.all_to_all(sent, ALL, 0, 0, axis_index_groups=PLANES, tiled=True)
    packed = attend(queries, key_cache, value_cache, new_key, new_value, lengths)
    weights = (w_gate[0].T, w_up[0].T, w_down[0])
    plane, packed, weights, expert = lax.optimization_barrier((plane, packed, weights, expert))
    plane = plane.reshape(64, D + META)
    shards = [plane] + [move(plane, OUTER, k) for k in (1, 2, 3)]

    gate_w, up_w, down_w = load(*weights)
    shards[1], gate_w = lax.optimization_barrier((shards[1], gate_w))

    chosen, own, other = [None] * 4, [None] * 4, [None] * 4
    for k in (0, 1, 3, 2):
        own[k], theirs, chosen[k] = choose(expert, shards[k])
        other[k] = move(theirs, CORE, 1)
    sums = expert_rows(expert, own, other, gate_w, up_w, down_w)

    parts = []
    for c in range(2):
        mine, theirs = sums[2 * c : 2 * c + 2]
        theirs = move(theirs, CORE, 1)
        rows = [give(chosen[k], mine, theirs, k) for k in (1, 3, 2)]
        if c == 1:
            rows[-1], packed = lax.optimization_barrier((rows[-1], packed))
        parts += [mine, theirs] + [move(r, OUTER, -k) for r, k in zip(rows, (1, 3, 2))]

    head_parts = lax.all_to_all(packed, "ctx", 0, 0, tiled=True)
    head_outputs = call(heads_kernel, shape(2, HD * QH // KVH), head_parts, name="heads")
    parts[-1], head_outputs = lax.optimization_barrier((parts[-1], head_outputs))
    sums = lax.all_to_all(
        join(chosen[0], parts), ALL, 0, 0, axis_index_groups=PLANES, tiled=True
    )
    return head_outputs, call(fold_kernel, shape(4, D), sums, name="fold")


def solution(mesh):
    placed = (
        P("grp", None),
        P("grp", "ctx", None),
        P("grp", "ctx", None),
        P("grp", None),
        P("grp", None),
        P("grp"),
        P(ALL, None),
        P(ALL, None),
        P(ALL, None),
        P("grp", None, "ctx"),
        P("grp", None, "ctx"),
        P("grp", "ctx", None),
    )
    return jax.shard_map(
        body,
        mesh=mesh,
        in_specs=placed,
        out_specs=(P("grp", "ctx"), P(ALL, None)),
        check_vma=False,
    )
```

```python
import functools

import jax
import jax.numpy as jnp
from jax import lax
from jax.experimental import pallas as pl
from jax.experimental.pallas import tpu as pltpu
from jax.sharding import PartitionSpec as P

QH = 48
KVH = 8
HD = 128
TOPK = 4
D = 6144
HALF = D // 2
FF = 672
META = 128
KB = 512
ALL = ("ctx", "grp")
BF = jnp.bfloat16
F32 = jnp.float32


def coords(i):
    c, g = divmod(i, 16)
    return {"x": (g >> 1) & 3, "y": c & 3, "z": ((g >> 3) << 1) | (c >> 2), "core": g & 1}


def index(x, y, z, core):
    return (((z & 1) << 2) | y) * 16 + (((z >> 1) << 3) | (x << 1) | core)


def shifted(axes, k):
    pairs = []
    for i in range(128):
        at = coords(i)
        axis = axes[at["core"]]
        at[axis] = (at[axis] + k) % (2 if axis == "core" else 4)
        pairs.append((i, index(**at)))
    return pairs


OUTER = ("x", "y")
INNER = ("y", "x")
CORE = ("core", "core")
PLANES = [
    [index(**{INNER[core]: i, OUTER[core]: o, "z": z, "core": core}) for i in range(4) for z in range(4)]
    for core in range(2)
    for o in range(4)
]


def move(a, axes, k):
    return lax.ppermute(a, ALL, shifted(axes, k % 4 if axes is not CORE else 1))


def call(kernel, outs, *args, name, limit=8, **kw):
    return pl.pallas_call(
        kernel,
        out_shape=outs,
        compiler_params=pltpu.CompilerParams(vmem_limit_bytes=limit << 20),
        cost_estimate=pl.CostEstimate(flops=0, bytes_accessed=0, transcendentals=0),
        name=name,
        **kw,
    )(*args)


VMEM = pl.BlockSpec(memory_space=pltpu.VMEM)
SMEM = pl.BlockSpec(memory_space=pltpu.SMEM)
HBM = pl.BlockSpec(memory_space=pltpu.HBM)


def in_hbm(*arrays):
    return [pltpu.with_memory_space_constraint(a, pltpu.HBM) for a in arrays]


def shape(*dims, dtype=BF):
    return jax.ShapeDtypeStruct(dims, dtype)


def pack_kernel(x_at, routes_at, weights_at, out, x, routes, weights, sems):
    copies = [
        pltpu.make_async_copy(a, b, sems.at[i])
        for i, (a, b) in enumerate(((x_at, x), (routes_at, routes), (weights_at, weights)))
    ]
    for copy in copies:
        copy.start()
    for copy in copies[1:]:
        copy.wait()
    row = lax.broadcasted_iota(jnp.int32, (4, TOPK), 0)
    place = lax.broadcasted_iota(jnp.int32, (4, TOPK), 1)
    named = jnp.zeros((4, TOPK), jnp.int32)
    for r in range(4):
        for k in range(TOPK):
            named = jnp.where((row == r) & (place == k), routes[r, k], named)
    code = 2 * named
    for r in range(3):
        for k in range(TOPK):
            code += jnp.where((named == routes[r, k]) & (row > r), 1, 0)
    share = weights[...] / jnp.sum(weights[...], axis=1, keepdims=True)
    high = share.astype(BF).astype(F32)
    middle = (share - high).astype(BF).astype(F32)
    lane = lax.broadcasted_iota(jnp.int32, (4, META), 1)
    meta = jnp.zeros((4, META), F32)
    for j, part in enumerate((code.astype(F32), high, middle, share - high - middle)):
        for k in range(TOPK):
            meta = jnp.where(lane == j * TOPK + k, part[:, k : k + 1], meta)
    meta = meta.astype(BF)
    for target in range(16):
        out[target, :, D:] = meta
    copies[0].wait()
    for target in range(16):
        out[target, :, :D] = x[...]


def pack(x, routes, weights):
    return call(
        pack_kernel,
        shape(16, 4, D + META),
        *in_hbm(x, routes, weights),
        name="pack",
        in_specs=[HBM] * 3,
        out_specs=VMEM,
        scratch_shapes=[
            pltpu.VMEM((4, D), BF),
            pltpu.SMEM((4, TOPK), jnp.int32),
            pltpu.VMEM((4, TOPK), F32),
            pltpu.SemaphoreType.DMA((3,)),
        ],
    )


def load_kernel(gate_at, up_at, down_at, gate, up, down, sems):
    parts = 3
    copies = []
    for i, (a, b) in enumerate(((gate_at, gate), (up_at, up), (down_at, down))):
        for p in range(parts):
            rows = pl.ds(p * (FF // parts), FF // parts)
            copies.append(pltpu.make_async_copy(a.at[rows], b.at[rows], sems.at[i, p]))
    for copy in copies:
        copy.start()
    for copy in copies:
        copy.wait()


def load(gate_w, up_w, down_w):
    return call(
        load_kernel,
        [pltpu.VMEM((FF, D), BF)] * 3,
        *in_hbm(gate_w, up_w, down_w),
        name="load",
        in_specs=[HBM] * 3,
        out_specs=[VMEM] * 3,
        scratch_shapes=[pltpu.SemaphoreType.DMA((3, 3))],
    )


def choose_kernel(expert, rows, mine, theirs, chosen):
    meta = rows[:, D:].astype(F32)
    row = lax.broadcasted_iota(jnp.int32, (64, 64), 0)
    lane = lax.broadcasted_iota(jnp.int32, (64, 64), 1)
    wanted = 2 * jnp.where(lane < 32, expert[0], expert[0] ^ 1) + lane % 2
    wanted = jnp.where(row // 4 == (lane % 32) // 2, wanted, -1).astype(F32)
    ones = jnp.zeros((64, 64), F32)
    for k in range(TOPK):
        ones += jnp.where(meta[:, k : k + 1] == wanted, 1.0, 0.0)
    chosen[...] = ones.astype(BF)
    for at in range(0, D + META, KB):
        here = slice(at, min(at + KB, D + META))
        found = lax.dot_general(
            chosen[...], rows[:, here], (((0,), (0,)), ((), ())), preferred_element_type=F32
        ).astype(BF)
        mine[:, here] = found[:32]
        theirs[:, here] = found[32:]


def choose(expert, rows):
    return call(
        choose_kernel,
        [shape(32, D + META), shape(32, D + META), shape(64, 64)],
        expert,
        rows,
        name="choose",
        in_specs=[SMEM, VMEM],
        out_specs=[VMEM] * 3,
    )


def across(weights, rows):
    return lax.dot_general(weights, rows, (((1,), (1,)), ((), ())), preferred_element_type=F32)


def expert_kernel(expert, *refs):
    picked, (gate_w, up_w, down_w, *outs) = refs[:8], refs[8:]
    rows = jnp.concatenate([r[:, :D] for r in picked], axis=0)
    meta = jnp.concatenate([r[:, D:] for r in picked], axis=0).astype(F32)
    share = jnp.zeros((256, 1), F32)
    for k in range(TOPK):
        of_row = sum(meta[:, j * TOPK + k : j * TOPK + k + 1] for j in (1, 2, 3))
        slot = meta[:, k : k + 1] - (2 * expert[0]).astype(F32)
        share += jnp.where((slot == 0.0) | (slot == 1.0), of_row, 0.0)
    gate, up = across(gate_w[...], rows), across(up_w[...], rows)
    hidden = ((gate / (1.0 + jnp.exp(-gate)) * up).T * share).astype(BF)
    for c in range(2):
        here = slice(c * HALF, (c + 1) * HALF)
        rows = jnp.dot(hidden, down_w[:, here], preferred_element_type=F32).astype(BF)
        outs[2 * c][...] = rows[:128]
        outs[2 * c + 1][...] = rows[128:]


def expert_rows(expert, own, other, gate_w, up_w, down_w):
    return call(
        expert_kernel,
        [shape(128, HALF)] * 4,
        expert,
        *own,
        *other,
        gate_w,
        up_w,
        down_w,
        name="expert",
        limit=16,
        in_specs=[SMEM] + [VMEM] * 11,
        out_specs=[VMEM] * 4,
    )


def given(chosen, mine, theirs, at):
    here = slice(at, at + KB)
    rows = jnp.concatenate([mine[:, here], theirs[:, here]], axis=0)
    return jnp.dot(chosen[...], rows, preferred_element_type=F32)


def give_kernel(chosen, mine, theirs, out):
    for at in range(0, HALF, KB):
        out[:, at : at + KB] = given(chosen, mine, theirs, at).astype(BF)


def give(chosen, mine, theirs, k):
    slots = pl.BlockSpec((32, HALF), lambda i: (k, 0))
    return call(
        give_kernel,
        shape(64, HALF),
        chosen,
        mine,
        theirs,
        name="give",
        grid=(1,),
        in_specs=[pl.BlockSpec((64, 64), lambda i: (0, 0)), slots, slots],
        out_specs=pl.BlockSpec((64, HALF), lambda i: (0, 0)),
    )


def join_kernel(chosen, *refs):
    parts, out = refs[:-1], refs[-1]
    for c in range(2):
        mine, theirs, *arrived = parts[5 * c : 5 * c + 5]
        for at in range(0, HALF, KB):
            rows = given(chosen, mine, theirs, at)
            for part in arrived:
                rows += part[:, at : at + KB].astype(F32)
            rows = rows.astype(BF)
            for block in range(16):
                out[block, :, c * HALF + at : c * HALF + at + KB] = rows[4 * block : 4 * block + 4]


def join(chosen, parts):
    slots = pl.BlockSpec((32, HALF), lambda i: (0, 0))
    rows = pl.BlockSpec((64, HALF), lambda i: (0, 0))
    return call(
        join_kernel,
        shape(16, 4, D),
        chosen,
        *parts,
        name="join",
        grid=(1,),
        in_specs=[pl.BlockSpec((64, 64), lambda i: (0, 0))] + [slots, slots, rows, rows, rows] * 2,
        out_specs=pl.BlockSpec((16, 4, D), lambda i: (0, 0, 0)),
    )


def fold_kernel(parts, out):
    out[...] = sum(parts[s].astype(F32) for s in range(16)).astype(BF)


def attend_kernel(place, lengths_at, *refs):
    given, out, held, sems = refs[:5], refs[5], refs[6:12], refs[12]
    copies = [
        pltpu.make_async_copy(a, b, sems.at[i]) for i, (a, b) in enumerate(zip((lengths_at,) + given, held))
    ]
    for copy in copies:
        copy.start()
    for copy in copies:
        copy.wait()
    lengths, queries, keys, values, new_key, new_value = held
    group = QH // KVH
    local = keys.shape[1]
    leader = place[0] == 0
    position = place[0] * local + lax.broadcasted_iota(jnp.int32, (group, local), 1)
    lane = lax.broadcasted_iota(jnp.int32, (group, HD), 1)
    out[...] = jnp.zeros_like(out)
    for r in range(2):
        live = position < lengths[r]
        for j in range(KVH):
            head = slice(j * HD, (j + 1) * HD)
            q = queries[r, j]
            scores = across(q, keys[r, :, head]) * HD ** (-0.5)
            own = jnp.sum(
                q.astype(F32) * new_key[r : r + 1, head].astype(F32), axis=1, keepdims=True
            ) * HD ** (-0.5)
            top = jnp.max(jnp.where(live, scores, -1e30), axis=1, keepdims=True)
            top = jnp.where(leader, jnp.maximum(top, own), top)
            top = top.astype(BF).astype(F32)
            weights = jnp.where(live, jnp.exp(scores - top), 0.0)
            own = jnp.where(leader, jnp.exp(own - top), 0.0)
            total = jnp.sum(weights, axis=1, keepdims=True) + own
            high = weights.astype(BF)
            low = (weights - high.astype(F32)).astype(BF)
            value = values[r, :, head]
            mixed = jnp.dot(high, value, preferred_element_type=F32)
            mixed += jnp.dot(low, value, preferred_element_type=F32)
            mixed += own * new_value[r : r + 1, head].astype(F32)
            total_high = total.astype(BF).astype(F32)
            stats = jnp.where(lane == 0, top, jnp.where(lane == 1, total_high, total - total_high))
            out[j, 8 * r : 8 * r + group, :HD] = mixed.astype(BF)
            out[j, 8 * r : 8 * r + group, HD:] = stats.astype(BF)


def attend(queries, key_cache, value_cache, new_key, new_value, lengths):
    place = lax.axis_index("ctx").astype(jnp.int32).reshape(1)
    queries = queries.reshape(2, KVH, QH // KVH, HD)
    return call(
        attend_kernel,
        shape(KVH, 16, 2 * HD),
        place,
        *in_hbm(lengths, queries, key_cache, value_cache, new_key, new_value),
        name="attend",
        in_specs=[SMEM] + [HBM] * 6,
        out_specs=VMEM,
        scratch_shapes=[pltpu.SMEM((2,), jnp.int32)]
        + [pltpu.VMEM(a.shape, a.dtype) for a in (queries, key_cache, value_cache, new_key, new_value)]
        + [pltpu.SemaphoreType.DMA((6,))],
    )


def heads_kernel(parts, out):
    group = QH // KVH
    tops = [parts[s, :, HD : HD + 1].astype(F32) for s in range(KVH)]
    peak = functools.reduce(jnp.maximum, tops)
    mixed = jnp.zeros((16, HD), F32)
    total = jnp.zeros((16, 1), F32)
    for s in range(KVH):
        scale = jnp.exp(tops[s] - peak)
        mixed += scale * parts[s, :, :HD].astype(F32)
        total += scale * sum(parts[s, :, HD + i : HD + i + 1].astype(F32) for i in (1, 2))
    mixed = (mixed / total).astype(BF)
    for r in range(2):
        for g in range(group):
            out[r : r + 1, g * HD : (g + 1) * HD] = mixed[8 * r + g : 8 * r + g + 1]


def body(
    queries,
    key_cache,
    value_cache,
    new_key,
    new_value,
    lengths,
    moe_input,
    routes,
    route_weights,
    w_gate,
    w_up,
    w_down,
):
    expert = lax.axis_index("grp").astype(jnp.int32).reshape(1)

    sent = pack(moe_input, routes, route_weights)
    plane = lax.all_to_all(sent, ALL, 0, 0, axis_index_groups=PLANES, tiled=True)
    packed = attend(queries, key_cache, value_cache, new_key, new_value, lengths)
    weights = (w_gate[0].T, w_up[0].T, w_down[0])
    plane, packed, weights, expert = lax.optimization_barrier((plane, packed, weights, expert))
    plane = plane.reshape(64, D + META)
    shards = [plane] + [move(plane, OUTER, k) for k in (1, 2, 3)]

    gate_w, up_w, down_w = load(*weights)
    shards[1], gate_w = lax.optimization_barrier((shards[1], gate_w))

    chosen, own, other = [None] * 4, [None] * 4, [None] * 4
    for k in (0, 1, 3, 2):
        own[k], theirs, chosen[k] = choose(expert, shards[k])
        other[k] = move(theirs, CORE, 1)
    sums = expert_rows(expert, own, other, gate_w, up_w, down_w)

    parts = []
    for c in range(2):
        mine, theirs = sums[2 * c : 2 * c + 2]
        theirs = move(theirs, CORE, 1)
        rows = [give(chosen[k], mine, theirs, k) for k in (1, 3, 2)]
        if c == 1:
            rows[-1], packed = lax.optimization_barrier((rows[-1], packed))
        parts += [mine, theirs] + [move(r, OUTER, -k) for r, k in zip(rows, (1, 3, 2))]

    head_parts = lax.all_to_all(packed, "ctx", 0, 0, tiled=True)
    head_outputs = call(heads_kernel, shape(2, HD * QH // KVH), head_parts, name="heads")
    parts[-1], head_outputs = lax.optimization_barrier((parts[-1], head_outputs))
    sums = lax.all_to_all(
        join(chosen[0], parts), ALL, 0, 0, axis_index_groups=PLANES, tiled=True
    )
    return head_outputs, call(fold_kernel, shape(4, D), sums, name="fold")


def solution(mesh):
    placed = (
        P("grp", None),
        P("grp", "ctx", None),
        P("grp", "ctx", None),
        P("grp", None),
        P("grp", None),
        P("grp"),
        P(ALL, None),
        P(ALL, None),
        P(ALL, None),
        P("grp", None, "ctx"),
        P("grp", None, "ctx"),
        P("grp", "ctx", None),
    )
    return jax.shard_map(
        body,
        mesh=mesh,
        in_specs=placed,
        out_specs=(P("grp", "ctx"), P(ALL, None)),
        check_vma=False,
    )
```
